32 devices in a mesh: rep: 2 (over y), fsdp: 16 (over z, x, core).
Axes of the slice: x: 2, y: 2, z: 4, core: 2. Of those that a mesh axis runs over, the one named last changes fastest.
Arguments:
- tracker: bfloat16 [2, 16, 128, 5120], P('rep', None, 'fsdp'), may hold values from -40 to 40
- levels: bfloat16 [2, 16, 128, 5120], P('rep', None, 'fsdp'), may hold values from -127 to 127, as said below
- exponents: int32 [2, 16, 128], P('rep', None, 'fsdp'), may hold values from -8 to -5
Outputs:
- update: bfloat16 [2, 16, 128, 5120], P('rep', None, 'fsdp')
The draws below stay inside these ranges and needn't reach their ends.
Inputs may be any that keep to these rules, and one draw needn't show every extreme that they name: `levels`: whole numbers.
All inputs are finite; a program needn't handle non-finite values.
Results may differ from the reference program's by a relative error of at most 0.025.
Values may be sent and summed in bfloat16 or wider, within the bound.
No kernel may reach another device: no remote copies, remote signals or barrier semaphores. Data moves between devices by JAX's collectives and lax.ppermute only.
A program may use at most 64 MiB of HBM per device.

```python
import math
import jax
import jax.numpy as jnp
from jax import lax

D = 5120
BR = 128
NS_STEPS = 5
REPLICAS = 2
MATS = 16


def draw_tracker(key, part):
    first = jax.random.fold_in(key, 11)
    second = jax.random.fold_in(key, 12)
    third = jax.random.fold_in(key, 13)
    base = jax.random.truncated_normal(first, -4.0, 4.0, (REPLICAS, MATS, BR, D), jnp.float32)
    half_log = 0.5 * math.log(10.0)
    row_scales = jnp.exp(jax.random.uniform(second, (REPLICAS, MATS, BR, 1), jnp.float32) * half_log)
    col_scales = jnp.exp(jax.random.uniform(third, (1, 1, 1, D), jnp.float32) * half_log)
    return (base * row_scales * col_scales).astype(jnp.bfloat16)


def draw_levels(key, part):
    drawn = jax.random.randint(jax.random.fold_in(key, 21), (REPLICAS, MATS, BR, D), -127, 128)
    return drawn.astype(jnp.float32).astype(jnp.bfloat16)


def set_ends(values, rng, least, high):
    index_at = [jax.random.randint(jax.random.fold_in(rng, axis), (), 0, length) for axis, length in enumerate(values.shape)]
    widest = values.shape.index(max(values.shape))
    neighbour = index_at[:widest] + [(index_at[widest] + 1) % values.shape[widest]] + index_at[widest + 1:]
    return values.at[tuple(index_at)].set(least).at[tuple(neighbour)].set(high)


def shard_levels(rng, dims, shards, low, top_value):
    def one(position, shards_of):
        draws = jax.random.uniform(jax.random.fold_in(jax.random.fold_in(rng, 6), position), (shards_of,), jnp.float32, low / len(shards), top_value / len(shards))
        return jnp.repeat(jnp.exp(draws), dims[position] // shards_of).reshape((-1,) + (1,) * (len(dims) - position - 1))

    level = one(*shards[0])
    for cut in shards[1:]:
        level = level * one(*cut)
    return level


def setup_inputs(seed: int = 0) -> dict:
    streams_of = jax.random.split(jax.random.key(seed), 4)
    tracker = draw_tracker(jax.random.fold_in(streams_of[3], 71), 0)
    levels = draw_levels(jax.random.fold_in(streams_of[3], 71), 0)
    exponents = set_ends(jax.random.randint(streams_of[2], (REPLICAS, MATS, BR), -8, -4), jax.random.fold_in(streams_of[2], 1), -8, (-4) - 1).astype(jnp.int32)
    return dict(tracker=tracker, levels=levels, exponents=exponents)


gamma_mix = 0.5
coef_a = 3.4445
coef_b = -4.775
coef_c = 2.0315

def newton_schulz(matrix):
    values = matrix.astype(jnp.float32)
    frobenius = jnp.sqrt(jnp.sum(values * values))
    iterate = (values / (frobenius + 1e-07)).astype(jnp.bfloat16)
    for iteration in range(NS_STEPS):
        gram_mat = jnp.dot(iterate, iterate.T, preferred_element_type=jnp.float32).astype(jnp.bfloat16)
        square = jnp.dot(gram_mat, gram_mat, preferred_element_type=jnp.float32)
        polynomial = (coef_b * gram_mat.astype(jnp.float32) + coef_c * square).astype(jnp.bfloat16)
        iterate = (coef_a * iterate.astype(jnp.float32) + jnp.dot(polynomial, iterate, preferred_element_type=jnp.float32)).astype(jnp.bfloat16)
    factor = 2.0 ** (int(math.log2(D)) // 2)
    return (iterate.astype(jnp.float32) * factor).astype(jnp.bfloat16)

def reference(tracker, levels, exponents):
    powers = jnp.exp2(exponents.astype(jnp.float32))[..., None]
    message = (levels.astype(jnp.float32) * powers).astype(jnp.bfloat16)
    from_left = jnp.roll(message, 1, axis=0).astype(jnp.float32)
    from_right = jnp.roll(message, -1, axis=0).astype(jnp.float32)
    mixed_rows = (tracker.astype(jnp.float32) + gamma_mix * (from_left + from_right - 2.0 * message.astype(jnp.float32))).astype(jnp.bfloat16)
    flat = mixed_rows.reshape(REPLICAS * MATS, BR, D)
    result = lax.map(newton_schulz, flat)
    return result.reshape(REPLICAS, MATS, BR, D)
```

```python
import math

import jax
import jax.numpy as jnp
from jax import lax
from jax.sharding import PartitionSpec as P

NS_STEPS = 5


gamma_mix = 0.5
coef_a = 3.4445
coef_b = -4.775
coef_c = 2.0315


def shifted(block, axis, distance):
    devices = range(lax.axis_size(axis))
    route = [((i - distance) % len(devices), i) for i in devices]
    return lax.ppermute(block, axis, route)


def orthogonalize(matrix, columns):
    values = matrix.astype(jnp.float32)
    frobenius = jnp.sqrt(jnp.sum(values * values))
    iterate = (values / (frobenius + 1e-07)).astype(jnp.bfloat16)
    for iteration in range(NS_STEPS):
        gram_mat = lax.dot_general(
            iterate, iterate, (((1,), (1,)), ((), ())), preferred_element_type=jnp.float32
        ).astype(jnp.bfloat16)
        square = jnp.dot(gram_mat, gram_mat, preferred_element_type=jnp.float32)
        polynomial = (coef_b * gram_mat.astype(jnp.float32) + coef_c * square).astype(jnp.bfloat16)
        iterate = (
            coef_a * iterate.astype(jnp.float32)
            + jnp.dot(polynomial, iterate, preferred_element_type=jnp.float32)
        ).astype(jnp.bfloat16)
    factor = 2.0 ** (int(math.log2(columns)) // 2)
    return (iterate.astype(jnp.float32) * factor).astype(jnp.bfloat16)


def per_device(tracker, levels, exponents):
    powers = jnp.exp2(exponents.astype(jnp.float32))[..., None]
    message = (levels.astype(jnp.float32) * powers).astype(jnp.bfloat16)
    from_left = shifted(message, "rep", 1)
    from_right = shifted(message, "rep", -1)
    mixed_rows = (
        tracker.astype(jnp.float32)
        + gamma_mix
        * (
            from_left.astype(jnp.float32)
            + from_right.astype(jnp.float32)
            - 2.0 * message.astype(jnp.float32)
        )
    ).astype(jnp.bfloat16)
    _, mats, rows, columns = tracker.shape
    owned_rows = lax.all_to_all(mixed_rows[0], "fsdp", split_axis=0, concat_axis=0, tiled=True)
    result = orthogonalize(owned_rows.reshape(mats * rows, columns), columns)
    result = result.reshape(mats, rows, columns)
    return lax.all_to_all(result, "fsdp", split_axis=0, concat_axis=0, tiled=True)[None]


def solution(mesh):
    in_specs = (P("rep", None, "fsdp", None), P("rep", None, "fsdp", None), P("rep", None, "fsdp"))
    out_specs = P("rep", None, "fsdp", None)
    return jax.shard_map(
        per_device, mesh=mesh, in_specs=in_specs, out_specs=out_specs, check_vma=False
    )
```

```python
import math
import jax
import jax.numpy as jnp
from jax import lax
from jax.sharding import PartitionSpec as P

NS_STEPS = 5
gamma_mix = 0.5
coef_a = 3.4445
coef_b = -4.775
coef_c = 2.0315


def shifted(block, axis, distance):
    devices = range(lax.axis_size(axis))
    route = [((i - distance) % len(devices), i) for i in devices]
    return lax.ppermute(block, axis, route)


def mix(tracker, message, left, right):
    f32 = jnp.float32
    return (
        tracker.astype(f32)
        + gamma_mix * (left.astype(f32) + right.astype(f32) - 2.0 * message.astype(f32))
    ).astype(jnp.bfloat16)


def orthogonalize(matrix, columns):
    values = matrix.astype(jnp.float32)
    frobenius = jnp.sqrt(jnp.sum(values * values))
    iterate = (values / (frobenius + 1e-07)).astype(jnp.bfloat16)
    for iteration in range(NS_STEPS):
        gram_mat = lax.dot_general(
            iterate, iterate, (((1,), (1,)), ((), ())), preferred_element_type=jnp.float32
        ).astype(jnp.bfloat16)
        square = jnp.dot(gram_mat, gram_mat, preferred_element_type=jnp.float32)
        polynomial = (coef_b * gram_mat.astype(jnp.float32) + coef_c * square).astype(jnp.bfloat16)
        iterate = (
            coef_a * iterate.astype(jnp.float32)
            + jnp.dot(polynomial, iterate, preferred_element_type=jnp.float32)
        ).astype(jnp.bfloat16)
    factor = 2.0 ** (int(math.log2(columns)) // 2)
    return (iterate.astype(jnp.float32) * factor).astype(jnp.bfloat16)


def per_device(tracker, levels, exponents):
    tracker, levels, exponents = tracker[0], levels[0], exponents[0]
    mats, rows, columns = tracker.shape
    half = mats // 2
    side = lax.axis_index("fsdp") // half
    halves = [list(range(half)), list(range(half, mats))]
    far = [(i, (i + half) % mats) for i in range(mats)]

    powers = jnp.exp2(exponents.astype(jnp.float32))[..., None]
    message = (levels.astype(jnp.float32) * powers).astype(jnp.bfloat16)

    def part(array, which):
        return lax.dynamic_slice_in_dim(array, which * half, half, 0)

    def within(array):
        return lax.all_to_all(array, "fsdp", 0, 0, axis_index_groups=halves, tiled=True)

    def gossip(piece):
        return piece, shifted(piece, "rep", 1), shifted(piece, "rep", -1)

    w = columns // 256 * 128
    far_message, far_tracker = part(message, 1 - side), part(tracker, 1 - side)
    g1 = gossip(far_message[..., :w])
    g2 = gossip(far_message[..., w:])
    g3 = gossip(part(message, side))
    far1 = mix(far_tracker[..., :w], *g1)
    _, g2 = lax.optimization_barrier((far1, g2))
    far2 = mix(far_tracker[..., w:], *g2)
    _, g3 = lax.optimization_barrier((far2, g3))
    far1 = lax.ppermute(far1, "fsdp", far)
    far2 = lax.ppermute(within(far2), "fsdp", far)
    near = mix(part(tracker, side), *g3)
    near, far1 = lax.optimization_barrier((near, far1))
    merged = within(jnp.concatenate([near, far1], axis=-1))
    near_rows = merged[..., :columns]
    far_rows = jnp.concatenate([merged[..., columns:], far2], axis=-1)
    owned = jnp.where(side == 0, jnp.concatenate([near_rows, far_rows], 0), jnp.concatenate([far_rows, near_rows], 0))
    result = orthogonalize(owned.reshape(mats * rows, columns), columns)
    result = result.reshape(mats, rows, columns)
    return lax.all_to_all(result, "fsdp", split_axis=0, concat_axis=0, tiled=True)[None]


def solution(mesh):
    in_specs = (P("rep", None, "fsdp", None), P("rep", None, "fsdp", None), P("rep", None, "fsdp"))
    out_specs = P("rep", None, "fsdp", None)
    return jax.shard_map(
        per_device, mesh=mesh, in_specs=in_specs, out_specs=out_specs, check_vma=False
    )
```

```python
import math
import jax
import jax.numpy as jnp
from jax import lax
from jax.sharding import PartitionSpec as P

NS_STEPS = 5
gamma_mix = 0.5
coef_a = 3.4445
coef_b = -4.775
coef_c = 2.0315


def shifted(block, axis, distance):
    devices = range(lax.axis_size(axis))
    route = [((i - distance) % len(devices), i) for i in devices]
    return lax.ppermute(block, axis, route)


def mix(tracker, message, left, right):
    f32 = jnp.float32
    return (
        tracker.astype(f32)
        + gamma_mix * (left.astype(f32) + right.astype(f32) - 2.0 * message.astype(f32))
    ).astype(jnp.bfloat16)


def orthogonalize(matrix, order, rows, columns):
    f32 = jnp.float32
    factor = 2.0 ** (int(math.log2(columns)) // 2)
    eye = jnp.eye(matrix.shape[0], dtype=f32)
    iterate = matrix
    for iteration in range(NS_STEPS):
        last = iteration == NS_STEPS - 1
        gram = lax.dot_general(iterate, iterate, (((1,), (1,)), ((), ())), preferred_element_type=f32)
        scale = 1.0
        if iteration == 0:
            gram = lax.optimization_barrier(gram)
            trace = jnp.broadcast_to(jnp.sum(gram * eye, axis=0, keepdims=True), (rows, gram.shape[1]))
            trace = jnp.sum(lax.optimization_barrier(trace), axis=1, keepdims=True)
            scale = jnp.tile(1.0 / (jnp.sqrt(trace) + 1e-07), (gram.shape[0] // rows, 1))
            gram = gram * (scale * scale)
        gram = gram.astype(jnp.bfloat16)
        square = jnp.dot(gram, gram, preferred_element_type=f32)
        polynomial = coef_b * gram.astype(f32) + coef_c * square
        if last:
            polynomial = order((coef_a * eye + polynomial) * factor).astype(jnp.bfloat16)
            return jnp.dot(polynomial, iterate, preferred_element_type=f32).astype(jnp.bfloat16)
        product = jnp.dot(polynomial.astype(jnp.bfloat16), iterate, preferred_element_type=f32)
        iterate = ((coef_a * iterate.astype(f32) + product) * scale).astype(jnp.bfloat16)


def per_device(tracker, levels, exponents):
    tracker, levels, exponents = tracker[0], levels[0], exponents[0]
    mats, rows, columns = tracker.shape
    half = mats // 2
    side = lax.axis_index("fsdp") // half
    halves = [list(range(half)), list(range(half, mats))]
    far = [(i, (i + half) % mats) for i in range(mats)]

    powers = jnp.exp2(exponents.astype(jnp.float32))[..., None]

    def dequantized(block, scale):
        return (block.astype(jnp.float32) * scale).astype(jnp.bfloat16)

    def part(array, which):
        return lax.dynamic_slice_in_dim(array, which * half, half, 0)

    def within(array):
        return lax.all_to_all(array, "fsdp", 0, 0, axis_index_groups=halves, tiled=True)

    def gossip(piece):
        return piece, shifted(piece, "rep", 1), shifted(piece, "rep", -1)

    w = columns // 256 * 128
    far_tracker1, far_tracker2 = part(tracker, 1 - side)[..., :w], part(tracker, 1 - side)[..., w:]
    near_tracker = part(tracker, side)
    far_powers = part(powers, 1 - side)
    message1 = dequantized(part(levels, 1 - side)[..., :w], far_powers)
    message1, levels = lax.optimization_barrier((message1, levels))
    message2 = dequantized(part(levels, 1 - side)[..., w:], far_powers)
    message3 = dequantized(part(levels, side), part(powers, side))
    far_tracker1, far_tracker2, near_tracker = lax.optimization_barrier((far_tracker1, far_tracker2, near_tracker))
    g1, g2, g3 = gossip(message1), gossip(message2), gossip(message3)
    far1 = mix(far_tracker1, *g1)
    _, g2 = lax.optimization_barrier((far1, g2))
    far2 = mix(far_tracker2, *g2)
    _, g3 = lax.optimization_barrier((far2, g3))
    far1 = lax.ppermute(far1, "fsdp", far)
    far2 = lax.ppermute(within(far2), "fsdp", far)
    near = mix(near_tracker, *g3)
    near, far1 = lax.optimization_barrier((near, far1))
    merged = within(jnp.concatenate([near, far1], axis=-1))
    near_rows = merged[..., :columns]
    far_rows = jnp.concatenate([merged[..., columns:], far2], axis=-1)
    owned = jnp.concatenate([near_rows, far_rows], 0).reshape(mats * rows, columns)
    owned = lax.optimization_barrier(owned)

    def order(square):
        return jnp.where(side == 0, square, jnp.roll(square, half * rows, axis=0))

    result = orthogonalize(owned, order, rows, columns)
    result = result.reshape(mats, rows, columns)
    return lax.all_to_all(result, "fsdp", split_axis=0, concat_axis=0, tiled=True)[None]


def solution(mesh):
    in_specs = (P("rep", None, "fsdp", None), P("rep", None, "fsdp", None), P("rep", None, "fsdp"))
    out_specs = P("rep", None, "fsdp", None)
    return jax.shard_map(
        per_device, mesh=mesh, in_specs=in_specs, out_specs=out_specs, check_vma=False
    )
```

```python
import math
import jax
import jax.numpy as jnp
from jax import lax
from jax.experimental import pallas as pl
from jax.experimental.pallas import tpu as pltpu
from jax.sharding import PartitionSpec as P

NS_STEPS = 5
gamma_mix = 0.5
coef_a = 3.4445
coef_b = -4.775
coef_c = 2.0315


def shifted(block, axis, distance):
    devices = range(lax.axis_size(axis))
    route = [((i - distance) % len(devices), i) for i in devices]
    return lax.ppermute(block, axis, route)


def mix(tracker, message, left, right):
    f32 = jnp.float32
    return (
        tracker.astype(f32)
        + gamma_mix * (left.astype(f32) + right.astype(f32) - 2.0 * message.astype(f32))
    ).astype(jnp.bfloat16)


def copy_kernel(block_ref, out_ref):
    out_ref[...] = block_ref[...]


def settle(block, flops):
    spec = pl.BlockSpec(memory_space=pltpu.VMEM)
    return pl.pallas_call(
        copy_kernel,
        out_shape=jax.ShapeDtypeStruct(block.shape, block.dtype),
        in_specs=[spec],
        out_specs=spec,
        cost_estimate=pl.CostEstimate(flops=flops, bytes_accessed=0, transcendentals=0),
    )(block)


def orthogonalize(matrix, order, rows, columns):
    f32 = jnp.float32
    factor = 2.0 ** (int(math.log2(columns)) // 2)
    eye = jnp.eye(matrix.shape[0], dtype=f32)
    iterate = matrix
    for iteration in range(NS_STEPS):
        last = iteration == NS_STEPS - 1
        gram = lax.dot_general(iterate, iterate, (((1,), (1,)), ((), ())), preferred_element_type=f32)
        scale = 1.0
        if iteration == 0:
            gram = lax.optimization_barrier(gram)
            trace = jnp.broadcast_to(jnp.sum(gram * eye, axis=0, keepdims=True), (rows, gram.shape[1]))
            trace = jnp.sum(lax.optimization_barrier(trace), axis=1, keepdims=True)
            scale = jnp.tile(1.0 / (jnp.sqrt(trace) + 1e-07), (gram.shape[0] // rows, 1))
            gram = gram * (scale * scale)
        gram = gram.astype(jnp.bfloat16)
        square = jnp.dot(gram, gram, preferred_element_type=f32)
        polynomial = coef_b * gram.astype(f32) + coef_c * square
        if last:
            polynomial = order((coef_a * eye + polynomial) * factor).astype(jnp.bfloat16)
            return jnp.dot(polynomial, iterate, preferred_element_type=f32).astype(jnp.bfloat16)
        product = jnp.dot(polynomial.astype(jnp.bfloat16), iterate, preferred_element_type=f32)
        iterate = ((coef_a * iterate.astype(f32) + product) * scale).astype(jnp.bfloat16)


def per_device(tracker, levels, exponents):
    tracker, levels, exponents = tracker[0], levels[0], exponents[0]
    mats, rows, columns = tracker.shape
    half = mats // 2
    side = lax.axis_index("fsdp") // half
    halves = [list(range(half)), list(range(half, mats))]
    far = [(i, i ^ (half + half // 2)) for i in range(mats)]

    def mirrored(block):
        return jnp.concatenate([block[half // 2 :], block[: half // 2]], 0)


    powers = jnp.exp2(exponents.astype(jnp.float32))[..., None]

    def dequantized(block, scale):
        return (block.astype(jnp.float32) * scale).astype(jnp.bfloat16)

    def part(array, which):
        return lax.dynamic_slice_in_dim(array, which * half, half, 0)

    def within(array):
        return lax.all_to_all(array, "fsdp", 0, 0, axis_index_groups=halves, tiled=True)

    def gossip(piece):
        return piece, shifted(piece, "rep", 1), shifted(piece, "rep", -1)

    w = columns * 13 // 20 // 128 * 128
    far_tracker1, far_tracker2 = part(tracker, 1 - side)[..., :w], mirrored(part(tracker, 1 - side)[..., w:])
    near_tracker = part(tracker, side)
    far_powers = part(powers, 1 - side)
    message1 = dequantized(part(levels, 1 - side)[..., :w], far_powers)
    message1, levels = lax.optimization_barrier((message1, levels))
    message2 = dequantized(mirrored(part(levels, 1 - side)[..., w:]), mirrored(far_powers))
    message3 = dequantized(part(levels, side), part(powers, side))
    far_tracker1, far_tracker2, near_tracker = lax.optimization_barrier((far_tracker1, far_tracker2, near_tracker))
    g1, g2, g3 = gossip(message1), gossip(message2), gossip(message3)
    far1 = mix(far_tracker1, *g1)
    _, g2 = lax.optimization_barrier((far1, g2))
    far2 = mix(far_tracker2, *g2)
    _, g3 = lax.optimization_barrier((far2, g3))
    far1 = lax.ppermute(far1, "fsdp", far)
    far2 = settle(lax.ppermute(within(far2), "fsdp", far), 20000000000)
    near = mix(near_tracker, *g3)
    near, far1 = lax.optimization_barrier((near, far1))
    merged = within(jnp.concatenate([near, far1], axis=-1))
    near_rows = merged[..., :columns]
    far_rows = jnp.concatenate([mirrored(merged[..., columns:]), far2], axis=-1)
    owned = jnp.concatenate([near_rows, far_rows], 0).reshape(mats * rows, columns)
    owned = lax.optimization_barrier(owned)

    def order(square):
        return jnp.where(side == 0, square, jnp.roll(square, half * rows, axis=0))

    result = orthogonalize(owned, order, rows, columns)
    result = result.reshape(mats, rows, columns)
    return lax.all_to_all(result, "fsdp", split_axis=0, concat_axis=0, tiled=True)[None]


def solution(mesh):
    in_specs = (P("rep", None, "fsdp", None), P("rep", None, "fsdp", None), P("rep", None, "fsdp"))
    out_specs = P("rep", None, "fsdp", None)
    return jax.shard_map(
        per_device, mesh=mesh, in_specs=in_specs, out_specs=out_specs, check_vma=False
    )
```

```python
import math
import jax
import jax.numpy as jnp
from jax import lax
from jax.experimental import pallas as pl
from jax.experimental.pallas import tpu as pltpu
from jax.sharding import PartitionSpec as P

NS_STEPS = 5
gamma_mix = 0.5
coef_a = 3.4445
coef_b = -4.775
coef_c = 2.0315


def shifted(block, axis, distance):
    devices = range(lax.axis_size(axis))
    route = [((i - distance) % len(devices), i) for i in devices]
    return lax.ppermute(block, axis, route)


def mix(tracker, message, left, right):
    f32 = jnp.float32
    return (
        tracker.astype(f32)
        + gamma_mix * (left.astype(f32) + right.astype(f32) - 2.0 * message.astype(f32))
    ).astype(jnp.bfloat16)


def copy_kernel(block_ref, out_ref):
    out_ref[...] = block_ref[...]


def settle(block, flops):
    spec = pl.BlockSpec(memory_space=pltpu.VMEM)
    return pl.pallas_call(
        copy_kernel,
        out_shape=jax.ShapeDtypeStruct(block.shape, block.dtype),
        in_specs=[spec],
        out_specs=spec,
        cost_estimate=pl.CostEstimate(flops=flops, bytes_accessed=0, transcendentals=0),
    )(block)


def orthogonalize(matrix, order, rows, columns):
    f32, bf16 = jnp.float32, jnp.bfloat16
    factor = 2.0 ** (int(math.log2(columns)) // 2)
    eye = jnp.eye(matrix.shape[0], dtype=f32)

    def dot(left, right):
        return jnp.dot(left.astype(bf16), right.astype(bf16), preferred_element_type=f32)

    def fine(left, right):
        return jnp.dot(left, right, precision=lax.Precision.HIGH, preferred_element_type=f32)

    def polynomial_of(gram):
        return coef_b * gram + coef_c * dot(gram, gram)

    def gram_of(block):
        return lax.dot_general(block, block, (((1,), (1,)), ((), ())), preferred_element_type=f32)

    gram = lax.optimization_barrier(gram_of(matrix))
    trace = jnp.broadcast_to(jnp.sum(gram * eye, axis=0, keepdims=True), (rows, gram.shape[1]))
    trace = jnp.sum(lax.optimization_barrier(trace), axis=1, keepdims=True)
    scale = jnp.tile(1.0 / (jnp.sqrt(trace) + 1e-07), (gram.shape[0] // rows, 1))
    gram = (gram * (scale * scale)).astype(bf16).astype(f32)
    first = polynomial_of(gram)
    step = coef_a * eye + first
    second = polynomial_of(fine(step, fine(gram, step)))
    both = coef_a * (first + second) + fine(second, first)
    product = jnp.dot((both * scale).astype(bf16), matrix, preferred_element_type=f32)
    iterate = ((coef_a * coef_a * scale) * matrix.astype(f32) + product).astype(bf16)
    for iteration in range(2, NS_STEPS):
        gram = gram_of(iterate).astype(bf16).astype(f32)
        polynomial = polynomial_of(gram)
        if iteration == NS_STEPS - 1:
            polynomial = order((coef_a * eye + polynomial) * factor).astype(bf16)
            polynomial = lax.optimization_barrier(polynomial)
            return jnp.dot(polynomial, iterate, preferred_element_type=f32).astype(bf16)
        product = jnp.dot(polynomial.astype(bf16), iterate, preferred_element_type=f32)
        iterate = (coef_a * iterate.astype(f32) + product).astype(bf16)


def per_device(tracker, levels, exponents):
    tracker, levels, exponents = tracker[0], levels[0], exponents[0]
    mats, rows, columns = tracker.shape
    half = mats // 2
    side = lax.axis_index("fsdp") // half
    halves = [list(range(half)), list(range(half, mats))]
    far = [(i, i ^ (half + half // 2)) for i in range(mats)]

    def mirrored(block):
        return jnp.concatenate([block[half // 2 :], block[: half // 2]], 0)


    powers = jnp.exp2(exponents.astype(jnp.float32))[..., None]

    def dequantized(block, scale):
        return (block.astype(jnp.float32) * scale).astype(jnp.bfloat16)

    def part(array, which):
        return lax.dynamic_slice_in_dim(array, which * half, half, 0)

    def within(array):
        return lax.all_to_all(array, "fsdp", 0, 0, axis_index_groups=halves, tiled=True)

    def gossip(piece):
        return piece, shifted(piece, "rep", 1), shifted(piece, "rep", -1)

    w = columns * 13 // 20 // 128 * 128
    far_tracker1, far_tracker2 = part(tracker, 1 - side)[..., :w], mirrored(part(tracker, 1 - side)[..., w:])
    near_tracker = part(tracker, side)
    far_powers = part(powers, 1 - side)
    message1 = dequantized(part(levels, 1 - side)[..., :w], far_powers)
    message1, levels = lax.optimization_barrier((message1, levels))
    message2 = dequantized(mirrored(part(levels, 1 - side)[..., w:]), mirrored(far_powers))
    message3 = dequantized(part(levels, side), part(powers, side))
    far_tracker1, far_tracker2, near_tracker = lax.optimization_barrier((far_tracker1, far_tracker2, near_tracker))
    g1, g2, g3 = gossip(message1), gossip(message2), gossip(message3)
    far1 = mix(far_tracker1, *g1)
    _, g2 = lax.optimization_barrier((far1, g2))
    far2 = mix(far_tracker2, *g2)
    _, g3 = lax.optimization_barrier((far2, g3))
    far1 = lax.ppermute(far1, "fsdp", far)
    far2 = settle(lax.ppermute(within(far2), "fsdp", far), 20000000000)
    near = mix(near_tracker, *g3)
    near, far1 = lax.optimization_barrier((near, far1))
    merged = within(jnp.concatenate([near, far1], axis=-1))
    near_rows = merged[..., :columns]
    far_rows = jnp.concatenate([mirrored(merged[..., columns:]), far2], axis=-1)
    owned = jnp.concatenate([near_rows, far_rows], 0).reshape(mats * rows, columns)
    owned = lax.optimization_barrier(owned)

    def order(square):
        return jnp.where(side == 0, square, jnp.roll(square, half * rows, axis=0))

    result = orthogonalize(owned, order, rows, columns)
    result = result.reshape(mats, rows, columns)
    return lax.all_to_all(result, "fsdp", split_axis=0, concat_axis=0, tiled=True)[None]


def solution(mesh):
    in_specs = (P("rep", None, "fsdp", None), P("rep", None, "fsdp", None), P("rep", None, "fsdp"))
    out_specs = P("rep", None, "fsdp", None)
    return jax.shard_map(
        per_device, mesh=mesh, in_specs=in_specs, out_specs=out_specs, check_vma=False
    )
```
